32 devices in a mesh: dp: 2 (over y), expert: 16 (over z, x, core).
Axes of the slice: x: 2, y: 2, z: 4, core: 2. Of those that a mesh axis runs over, the one named last changes fastest.
Arguments:
- hidden: bfloat16 [16384, 1024], P(('dp', 'expert')), may hold values from -6 to 6
- segments: int32 [16384], P(('dp', 'expert')), may hold values from 0 to 16, never falling along the last dimension, each value on 1 to 2000 neighbouring positions
- routes: int32 [16384, 8], P(('dp', 'expert')), may hold values from 0 to 15, all different within a row
- capacity_blocks: int32 [16], replicated, may hold values from 1 to 2, as said below
- attn_gain: bfloat16 [1024], P('dp'), may hold values from 0.5 to 1.5
- w_query: bfloat16 [1024, 1024], P('dp'), may hold values from -0.375 to 0.375
- key_value_weight: bfloat16 [1024, 1024], P('dp'), may hold values from -0.1875 to 0.1875
- w_out: bfloat16 [1024, 1024], P('dp'), may hold values from -1.5 to 1.5
- ffn_gain: bfloat16 [1024], P('dp'), may hold values from 0.5 to 1.5
- w_router: bfloat16 [1024, 16], P('dp'), may hold values from -0.09375 to 0.09375
- expert_in: bfloat16 [16, 1024, 1024], P('expert', 'dp'), may hold values from -0.1875 to 0.1875
- expert_down: bfloat16 [16, 1024, 512], P('expert', 'dp'), may hold values from -0.75 to 0.75
- cotangent: bfloat16 [16384, 1024], P(('dp', 'expert')), may hold values from -6 to 6
Outputs:
- block_out: bfloat16 [16384, 1024], P(('dp', 'expert'))
- hidden_grad: bfloat16 [16384, 1024], P(('dp', 'expert'))
- attn_gain_grad: float32 [1024], P('dp')
- query_grad: float32 [1024, 1024], P('dp')
- keyval_grad: float32 [1024, 1024], P('dp')
- out_grad: float32 [1024, 1024], P('dp')
- ffn_gain_grad: float32 [1024], P('dp')
- router_grad: float32 [1024, 16], P('dp')
- expert_in_grad: float32 [16, 1024, 1024], P('expert', 'dp')
- expert_down_grad: float32 [16, 1024, 512], P('expert', 'dp')
The draws below stay inside these ranges and needn't reach their ends.
Inputs may be any that keep to these rules, and one draw needn't show every extreme that they name: `capacity_blocks`: some expert has 1 block and some has 2; a pair beyond its expert's capacity within its sequence is dropped.
All inputs are finite; a program needn't handle non-finite values.
Results may differ from the reference program's by a relative error of at most 0.02.
The reference program's roundings to bfloat16 on the way count: a program that leaves them out, or rounds other values in their place, can miss the bound.
Values may be sent and summed in bfloat16 or wider, within the bound.
A program may use at most 320 MiB of HBM per device.

```python
import math
import jax
import jax.numpy as jnp
import numpy as np
from jax import lax

MODEL_DIMENSION = 1024
QUERY_HEADS = 16
KEY_VALUE_HEADS = 8
HEAD_DIMENSION = 64
FF = 512
TOPK = 8
TOKENS_PER_PART = 512
BLOCK_ROWS = 128
CB = 2
DOC_MOST = 2000
EXPERTS = 16
TOKENS = 16384
DOCS = 17


def draw_capacity_blocks(key, part):
    key = jax.random.fold_in(key, 7)
    key_count, key_full, key_empty = jax.random.split(key, 3)
    counts = jax.random.randint(key_count, (EXPERTS,), 1, CB + 1)
    fullest = jax.random.randint(key_full, (), 0, EXPERTS)
    offset = jax.random.randint(key_empty, (), 1, EXPERTS)
    emptiest = (fullest + offset) % EXPERTS
    expert_ids = jnp.arange(EXPERTS)
    counts = jnp.where(expert_ids == fullest, CB, counts)
    counts = jnp.where(expert_ids == emptiest, 1, counts)
    return counts.astype(jnp.int32)


def steps_of(key, dims, cuts, low, high):
    factor_of = 1.0
    for dim, parts in cuts:
        steps = jax.random.uniform(jax.random.fold_in(jax.random.fold_in(key, 6), dim), (parts,), jnp.float32, low / len(cuts), high / len(cuts))
        factor_of = factor_of * jnp.repeat(jnp.exp(steps), dims[dim] // parts).reshape((-1,) + (1,) * (len(dims) - 1 - dim))
    return factor_of


def choose_distinct(key, rows, amount, top, lift):
    sequence = jax.random.permutation(jax.random.fold_in(key, 1), amount)
    pull = sequence
    for power in range(3):
        pull = pull * pull // amount
    pull = pull * lift // amount
    lots = jax.random.randint(jax.random.fold_in(key, 2), (rows, amount), 0, 4096) + pull
    fixed_rows = jax.random.permutation(jax.random.fold_in(key, 3), rows)[jnp.arange(amount) % rows]
    lots = jnp.where(jnp.arange(rows)[:, None] == fixed_rows[None, :], 1 << 14, lots)
    score = lots * amount + jnp.arange(amount)
    return lax.top_k(score.astype(jnp.int32), top)[1].astype(jnp.int32)


def length_profile(number_of, total, bound, slope):
    weights = [(1 << 20) // math.isqrt(standing ** slope) + 1 for standing in range(2, number_of + 1)]
    surplus, holding = total - bound - (number_of - 1), [1] * (number_of - 1)
    while surplus > 0:
        candidates = [i for i in range(number_of - 1) if holding[i] < bound]
        pool, budget = sum([weights[i] for i in candidates]), surplus
        for i in candidates:
            addition = min(bound - holding[i], max(1, budget * weights[i] // pool), surplus)
            holding[i] = holding[i] + addition
            surplus = surplus - addition
    return np.array([bound] + holding)


def uneven_parts(own_key, amount, total, bound, skew):
    if amount == 2:
        one = jax.random.randint(own_key, (), max(1, total - bound), min(bound, total - 1) + 1)
        return jnp.stack([one, total - one])
    lengths = jnp.asarray(length_profile(amount, total, bound, skew), jnp.int32)
    twos = (amount - 1) // 2
    giver, taker = lengths[1:1 + 2 * twos:2], lengths[2:2 + 2 * twos:2]
    slack = jnp.minimum(giver - 1, bound - taker)
    shifted = jax.random.randint(jax.random.fold_in(own_key, 1), (twos,), 0, 1 << 20) % (slack + 1)
    lengths = lengths.at[1:1 + 2 * twos:2].set(giver - shifted).at[2:2 + 2 * twos:2].set(taker + shifted)
    return lengths[jax.random.permutation(jax.random.fold_in(own_key, 2), amount)]


def normal_values(key, dims, spread, limit, shards=(), kind=jnp.bfloat16):
    loudness = steps_of(key, dims, shards, -0.22, 0.18) if shards else 1.0
    entries = jax.random.normal(key, dims, jnp.float32) * spread * loudness
    return jnp.minimum(jnp.maximum(entries, -limit), limit).astype(kind)


def setup_inputs(seed: int = 0) -> dict:
    splits = jax.random.split(jax.random.key(seed), 14)
    hidden = normal_values(splits[0], (TOKENS, MODEL_DIMENSION), 1.0, 6.0, ((0, 32),))
    segments = jnp.searchsorted(jnp.cumsum(uneven_parts(splits[1], DOCS, TOKENS, DOC_MOST, 1)), jnp.arange(TOKENS), side="right").astype(jnp.int32)
    routes = choose_distinct(splits[2], TOKENS, EXPERTS, TOPK, 4096)
    capacity_blocks = draw_capacity_blocks(jax.random.fold_in(splits[13], 71), 0)
    attn_gain = jnp.clip(1.0 + 0.1 * jax.random.normal(splits[4], (MODEL_DIMENSION,), jnp.float32), 0.5, 1.5).astype(jnp.bfloat16)
    w_query = normal_values(splits[5], (MODEL_DIMENSION, QUERY_HEADS * HEAD_DIMENSION), (MODEL_DIMENSION // 4) ** -0.5, 0.375, ((0, 2),))
    key_value_weight = normal_values(splits[6], (MODEL_DIMENSION, 2 * KEY_VALUE_HEADS * HEAD_DIMENSION), MODEL_DIMENSION ** -0.5, 0.1875, ((0, 2),))
    w_out = normal_values(splits[7], (QUERY_HEADS * HEAD_DIMENSION, MODEL_DIMENSION), (max(QUERY_HEADS * HEAD_DIMENSION // 64, 1)) ** -0.5, 1.5, ((0, 2),))
    ffn_gain = jnp.clip(1.0 + 0.1 * jax.random.normal(splits[8], (MODEL_DIMENSION,), jnp.float32), 0.5, 1.5).astype(jnp.bfloat16)
    w_router = normal_values(splits[9], (MODEL_DIMENSION, EXPERTS), (4 * MODEL_DIMENSION) ** -0.5, 0.09375, ((0, 2),))
    expert_in = normal_values(splits[10], (EXPERTS, MODEL_DIMENSION, 2 * FF), MODEL_DIMENSION ** -0.5, 0.1875, ((0, 16), (1, 2)))
    expert_down = normal_values(splits[11], (EXPERTS, MODEL_DIMENSION, FF), (FF // 8) ** -0.5, 0.75, ((0, 16), (1, 2)))
    cotangent = normal_values(splits[12], (TOKENS, MODEL_DIMENSION), 1.0, 6.0, ((0, 32),))
    return {"hidden": hidden, "segments": segments, "routes": routes, "capacity_blocks": capacity_blocks, "attn_gain": attn_gain, "w_query": w_query, "key_value_weight": key_value_weight, "w_out": w_out, "ffn_gain": ffn_gain, "w_router": w_router, "expert_in": expert_in, "expert_down": expert_down, "cotangent": cotangent}


@jax.custom_vjp
def reduced_precision(v):
    return lax.optimization_barrier(v.astype(jnp.bfloat16)).astype(jnp.float32)

@jax.custom_vjp
def low_back(v):
    return v

def low_keep(v):
    return (reduced_precision(v), None)

def low_pass(kept, grad):
    return (grad,)

def back_keep(v):
    return (v, None)

def back_low(kept, grad):
    return (reduced_precision(grad),)
reduced_precision.defvjp(low_keep, low_pass)
low_back.defvjp(back_keep, back_low)
highest = lax.Precision.HIGHEST
norm_eps = 1e-06
theta_base = 10000.0

def matmul(left, right):
    return jnp.dot(left, right, precision=highest, preferred_element_type=jnp.float32)

def rms_norm(value, gain_vec):
    return value * lax.rsqrt(lax.optimization_barrier(jnp.mean(value * value, axis=-1, keepdims=True)) + norm_eps) * gain_vec

def rotary_tables(sequence_length, head_dim):
    half_dim = head_dim // 2
    inverse = theta_base ** (-jnp.arange(half_dim, dtype=jnp.float32) * 2.0 / head_dim)
    angles = jnp.arange(sequence_length, dtype=jnp.float32)[:, None] * inverse[None, :]
    angles = jnp.concatenate([angles, angles], axis=-1)
    return (jnp.cos(angles), jnp.sin(angles))

def apply_rotation(value, cosine_lookup, sine_lookup):
    half_dim = value.shape[-1] // 2
    turned = jnp.concatenate([-value[..., half_dim:], value[..., :half_dim]], axis=-1)
    return value * cosine_lookup[:, None, :] + turned * sine_lookup[:, None, :]

def attend(pieces):
    query_rows, key_row_list, value_row_list, seg_ids = pieces
    sequence_length = query_rows.shape[0]
    grouped_heads = query_rows.reshape(sequence_length, KEY_VALUE_HEADS, QUERY_HEADS // KEY_VALUE_HEADS, HEAD_DIMENSION)
    scores = jnp.einsum('qkgd,skd->kgqs', grouped_heads, key_row_list, precision=highest) * HEAD_DIMENSION ** (-0.5)
    scores = low_back(scores)
    positions = jnp.arange(sequence_length, dtype=jnp.int32)
    allowed = (positions[:, None] >= positions[None, :]) & (seg_ids[:, None] == seg_ids[None, :])
    masked = jnp.where(allowed[None, None], scores, -1e+30)
    probability = reduced_precision(jax.nn.softmax(masked, axis=-1))
    mixed = jnp.einsum('kgqs,skd->qkgd', probability, value_row_list, precision=highest)
    return mixed.reshape(sequence_length, QUERY_HEADS * HEAD_DIMENSION)

def expert_term(carry, pieces):
    moe_in, w_in, w_down, column = (pieces[0], pieces[1], pieces[2], pieces[3])
    routed = low_back(moe_in)
    gate_up = low_back(matmul(routed, w_in))
    gate_part = gate_up[:, :FF]
    up_part = gate_up[:, FF:]
    expert_hidden = reduced_precision(jax.nn.silu(gate_part) * up_part)
    expert_out = reduced_precision(low_back(matmul(expert_hidden, w_down.T)))
    return carry + expert_out * column[:, None]

def layer_forward(resid_in, weights, seg_part, kept_part, route_part):
    attn_gain, w_query, key_value_weight, w_out, ffn_gain, w_router, expert_in, expert_down = weights
    local_sequences = seg_part.shape[0]
    normed = reduced_precision(rms_norm(resid_in, attn_gain))
    query_pre = low_back(matmul(normed, w_query))
    key_value_projected = low_back(matmul(normed, key_value_weight))
    key_columns = KEY_VALUE_HEADS * HEAD_DIMENSION
    cosine_lookup, sine_lookup = rotary_tables(TOKENS_PER_PART, HEAD_DIMENSION)
    query_rows = reduced_precision(jax.vmap(lambda block_value: apply_rotation(block_value, cosine_lookup, sine_lookup))(query_pre.reshape(local_sequences, TOKENS_PER_PART, QUERY_HEADS, HEAD_DIMENSION)))
    key_row_list = reduced_precision(jax.vmap(lambda block_value: apply_rotation(block_value, cosine_lookup, sine_lookup))(key_value_projected[:, :key_columns].reshape(local_sequences, TOKENS_PER_PART, KEY_VALUE_HEADS, HEAD_DIMENSION)))
    value_row_list = reduced_precision(key_value_projected[:, key_columns:].reshape(local_sequences, TOKENS_PER_PART, KEY_VALUE_HEADS, HEAD_DIMENSION))
    attended = lax.map(jax.checkpoint(attend), (query_rows, key_row_list, value_row_list, seg_part))
    attended = reduced_precision(low_back(attended.reshape(local_sequences * TOKENS_PER_PART, QUERY_HEADS * HEAD_DIMENSION)))
    branch_out = low_back(matmul(attended, w_out))
    first_sum = resid_in + branch_out
    moe_in = reduced_precision(rms_norm(first_sum, ffn_gain))
    logits = low_back(matmul(moe_in, w_router))
    expert_count = w_router.shape[1]
    choice_hot = (route_part[:, :, None] == jnp.arange(expert_count, dtype=jnp.int32)[None, None, :]).astype(jnp.float32)
    selected = lax.optimization_barrier(jnp.sum(choice_hot * logits[:, None, :], axis=-1))
    gates = jax.nn.softmax(selected, axis=-1)
    coefficient = lax.optimization_barrier(jnp.sum(choice_hot * (gates * kept_part)[:, :, None], axis=1))

    def scan_body(carry, pieces):
        return (expert_term(carry, (moe_in, pieces[0], pieces[1], pieces[2])), None)
    mixture, unused = lax.scan(jax.checkpoint(scan_body), jnp.zeros_like(first_sum), (expert_in, expert_down, coefficient.T))
    return first_sum + mixture

def capacity_mask(routes, capacity_blocks, devices):
    expert_count = capacity_blocks.shape[0]
    flat_routes = routes.reshape(devices, TOKENS_PER_PART * TOPK)
    hot_table = (flat_routes[:, :, None] == jnp.arange(expert_count, dtype=jnp.int32)[None, None, :]).astype(jnp.int32)
    ranks = lax.optimization_barrier(jnp.sum(jnp.cumsum(hot_table, axis=1).astype(jnp.int32) * hot_table, axis=-1)).astype(jnp.int32) - 1
    limits = BLOCK_ROWS * lax.optimization_barrier(jnp.sum(hot_table * capacity_blocks[None, None, :], axis=-1)).astype(jnp.int32)
    return (ranks < limits).astype(jnp.float32).reshape(devices * TOKENS_PER_PART, TOPK)

def add_up(first_val, second_val):
    return first_val + second_val

def reference(hidden, segments, routes, capacity_blocks, attn_gain, w_query, key_value_weight, w_out, ffn_gain, w_router, expert_in, expert_down, cotangent):
    devices = hidden.shape[0] // TOKENS_PER_PART
    per_group = math.gcd(devices, max(1, 4096 // TOKENS_PER_PART))
    groups = devices // per_group
    group_rows = per_group * TOKENS_PER_PART
    model_width = hidden.shape[1]
    kept_mask = capacity_mask(routes, capacity_blocks, devices)
    weights = tuple((arr.astype(jnp.float32) for arr in (attn_gain, w_query, key_value_weight, w_out, ffn_gain, w_router, expert_in, expert_down)))
    inputs = (hidden.astype(jnp.float32).reshape(groups, group_rows, model_width), segments.reshape(groups, per_group, TOKENS_PER_PART), kept_mask.reshape(groups, group_rows, TOPK), routes.reshape(groups, group_rows, TOPK), cotangent.astype(jnp.float32).reshape(groups, group_rows, model_width))

    def scan_step(totals, group_data):
        x_part, seg_part, kept_part, route_part, cot_part = group_data

        def forward_fn(x_value, weight_values):
            return layer_forward(x_value, weight_values, seg_part, kept_part, route_part)
        result, pull_back = jax.vjp(forward_fn, x_part, weights)
        x_grad, weight_grads = pull_back(cot_part)
        totals = jax.tree.map(add_up, totals, weight_grads)
        return (totals, (result.astype(jnp.bfloat16), x_grad.astype(jnp.bfloat16)))
    zero_grads = jax.tree.map(jnp.zeros_like, weights)
    totals, (outputs, input_grads) = lax.scan(scan_step, zero_grads, inputs)
    block_out = outputs.reshape(devices * TOKENS_PER_PART, model_width)
    hidden_grad = input_grads.reshape(devices * TOKENS_PER_PART, model_width)
    return (block_out, hidden_grad, totals[0], totals[1], totals[2], totals[3], totals[4], totals[5], totals[6], totals[7])
```

```python
import jax
import jax.numpy as jnp
from jax import lax
from jax.sharding import PartitionSpec as P

QUERY_HEADS = 16
KEY_VALUE_HEADS = 8
HEAD_DIMENSION = 64
FF = 512
BLOCK_ROWS = 128
CB = 2


norm_eps = 1e-06
theta_base = 10000.0


def rotary_tables(sequence_length, head_dim):
    half_dim = head_dim // 2
    inverse = theta_base ** (-jnp.arange(half_dim, dtype=jnp.float32) * 2.0 / head_dim)
    angles = jnp.arange(sequence_length, dtype=jnp.float32)[:, None] * inverse[None, :]
    angles = jnp.concatenate([angles, angles], axis=-1)
    return (jnp.cos(angles), jnp.sin(angles))


def apply_rotation(value, cosine_lookup, sine_lookup):
    half_dim = value.shape[-1] // 2
    turned = jnp.concatenate([-value[..., half_dim:], value[..., :half_dim]], axis=-1)
    return value * cosine_lookup[:, None, :] + turned * sine_lookup[:, None, :]


def unrotate(grad_val, cosine_lookup, sine_lookup):
    half_dim = grad_val.shape[-1] // 2
    scaled = grad_val * sine_lookup[:, None, :]
    turned = jnp.concatenate([scaled[..., half_dim:], -scaled[..., :half_dim]], axis=-1)
    return grad_val * cosine_lookup[:, None, :] + turned


def masked_scores(query_block, key_rot, block_start, seg_ids, scale):
    span_len = query_block.shape[0]
    raw_scores = (
        jnp.einsum("qkgd,skd->kgqs", query_block, key_rot, preferred_element_type=jnp.float32)
        * scale
    )
    query_pos = block_start + jnp.arange(span_len, dtype=jnp.int32)
    key_pos = jnp.arange(key_rot.shape[0], dtype=jnp.int32)
    allowed = (query_pos[:, None] >= key_pos[None, :]) & (seg_ids[:, None] == seg_ids[None, :])
    return jnp.where(allowed[None, None], raw_scores, -1e30)


def norm_backward(grad_in, gain_vec, normalized, inverse_rms):
    scaled = grad_in * gain_vec
    return inverse_rms * (
        scaled - normalized * jnp.mean(scaled * normalized, axis=-1, keepdims=True)
    )


def at_offset(arr, owners, dz, dx, dc):
    pairs = []
    for i in range(owners):
        z, x, c = i // 4, (i // 2) % 2, i % 2
        source = (((z + dz) % (owners // 4)) * 2 + (x ^ dx)) * 2 + (c ^ dc)
        pairs.append((source, i))
    return lax.ppermute(arr, "expert", pairs)


def swap_dp(arr):
    return lax.ppermute(arr, "dp", [(0, 1), (1, 0)])


def piece(arr, index, size, axis=0):
    return lax.dynamic_slice_in_dim(arr, index * size, size, axis)


def in_order(first, mine, other, axis=0):
    return jnp.where(
        first, jnp.concatenate([mine, other], axis), jnp.concatenate([other, mine], axis)
    )


def add_low(left, right):
    return (left.astype(jnp.float32) + right.astype(jnp.float32)).astype(jnp.bfloat16)


def gather_rows(arr, owners):
    across = owners // 4
    got = {(0, 0, 0): arr}
    got[0, 1, 0] = at_offset(arr, owners, 0, 1, 0)
    order = sorted(range(1, across), key=lambda k: min(k, across - k))
    for k in order:
        got[k, 0, 0] = at_offset(arr, owners, k, 0, 0)
    for k in order:
        got[k, 1, 0] = at_offset(got[k, 0, 0], owners, 0, 1, 0)
    for k in [0] + order:
        for x in range(2):
            got[k, x, 1] = at_offset(got[k, x, 0], owners, 0, 0, 1)
    return got


def scatter_rows(parts, owners):
    across = owners // 4
    order = sorted(range(1, across), key=lambda k: min(k, across - k))
    total = None
    for k in order + [0]:
        far = add_low(parts[k, 1, 0], at_offset(parts[k, 1, 1], owners, 0, 0, 1))
        near = add_low(parts[k, 0, 0], at_offset(parts[k, 0, 1], owners, 0, 0, 1))
        row = add_low(near, at_offset(far, owners, 0, 1, 0))
        if k:
            row = at_offset(row, owners, across - k, 0, 0)
        row = row.astype(jnp.float32)
        total = row if total is None else total + row
    return total


def whole_rows(arr, owners):
    if lax.axis_size("dp") != 2:
        return lax.all_gather(arr, "dp", axis=0, tiled=True)
    core = lax.axis_index("expert") % 2
    got = swap_dp(piece(arr, core, arr.shape[0] // 2))
    other = in_order(core == 0, got, at_offset(got, owners, 0, 0, 1))
    return in_order(lax.axis_index("dp") == 0, arr, other)


def whole_expert(arr):
    if lax.axis_size("dp") != 2:
        return lax.all_gather(arr, "dp", axis=0, tiled=True)
    return in_order(lax.axis_index("dp") == 0, arr, swap_dp(arr))


def fold_expert(grad):
    if lax.axis_size("dp") != 2:
        return lax.psum_scatter(
            grad.astype(jnp.bfloat16), "dp", scatter_dimension=0, tiled=True
        ).astype(jnp.float32)
    side = lax.axis_index("dp")
    half = grad.shape[0] // 2
    sent = swap_dp(piece(grad, 1 - side, half).astype(jnp.bfloat16))
    return piece(grad, side, half) + sent.astype(jnp.float32)


def fold_shared(grad, owners):
    low = grad.astype(jnp.bfloat16)
    if lax.axis_size("dp") != 2:
        return lax.psum_scatter(
            lax.psum(low, "expert"), "dp", scatter_dimension=0, tiled=True
        ).astype(jnp.float32)
    me = lax.axis_index("expert")
    z, x, c = me // 4, (me // 2) % 2, me % 2
    side = lax.axis_index("dp")
    across = owners // 4
    wide = low.shape[1] // 2
    low = add_low(
        piece(low, c, wide, 1), at_offset(piece(low, 1 - c, wide, 1), owners, 0, 0, 1)
    )
    half = low.shape[0] // 2
    low = add_low(piece(low, side, half), swap_dp(piece(low, 1 - side, half)))
    quarter = half // 2
    low = add_low(piece(low, x, quarter), at_offset(piece(low, 1 - x, quarter), owners, 0, 1, 0))
    rows = quarter // across
    total = piece(low, z, rows).astype(jnp.float32)
    for k in range(1, across):
        sent = at_offset(piece(low, (z + across - k) % across, rows), owners, k, 0, 0)
        total = total + sent.astype(jnp.float32)
    low = total.astype(jnp.bfloat16)
    turned = [low] + [at_offset(low, owners, k, 0, 0) for k in range(1, across)]
    low = lax.dynamic_slice_in_dim(
        jnp.concatenate(turned + turned, 0), ((across - z) % across) * rows, quarter, 0
    )
    low = in_order(x == 0, low, at_offset(low, owners, 0, 1, 0))
    low = in_order(c == 0, low, at_offset(low, owners, 0, 0, 1), 1)
    return low.astype(jnp.float32)


def on_device(
    hidden,
    segments,
    routes,
    capacity_blocks,
    attn_gain,
    w_query,
    key_value_weight,
    w_out,
    ffn_gain,
    w_router,
    expert_in,
    expert_down,
    cotangent,
):
    sequence_length = hidden.shape[0]
    model_width = hidden.shape[1]
    expert_count = capacity_blocks.shape[0]
    owners = lax.axis_size("expert")
    across = owners // 4
    capacity = BLOCK_ROWS * CB
    group_length = QUERY_HEADS // KEY_VALUE_HEADS
    key_columns = KEY_VALUE_HEADS * HEAD_DIMENSION
    scale = HEAD_DIMENSION ** (-0.5)
    brain_float_half = jnp.bfloat16
    single_float = jnp.float32
    small = lax.all_gather(
        jnp.concatenate([attn_gain[None], ffn_gain[None], w_router.T], axis=0),
        "dp",
        axis=1,
        tiled=True,
    )
    gain_attn = small[0].astype(single_float)
    gain_ffn = small[1].astype(single_float)
    full_router = small[2:].T
    full_query = whole_rows(w_query, owners)
    full_keyval = whole_rows(key_value_weight, owners)
    full_out = whole_rows(w_out, owners)
    expert_ids = jnp.arange(expert_count, dtype=jnp.int32)
    routed = jnp.any(routes[:, :, None] == expert_ids[None, None, :], axis=1)
    earlier = (
        jnp.arange(sequence_length)[:, None] > jnp.arange(sequence_length)[None, :]
    ).astype(brain_float_half)
    ranks = jnp.dot(
        earlier, routed.astype(brain_float_half), preferred_element_type=single_float
    )
    kept_mask = routed & (ranks < (BLOCK_ROWS * capacity_blocks[None, :]).astype(single_float))
    slots = jnp.where(kept_mask, ranks, -1.0)
    me = lax.axis_index("expert")
    offsets = [(k, x, c) for k in range(across) for x in range(2) for c in range(2)]
    sources = jnp.stack(
        [(((me // 4 + k) % across) * 2 + ((me // 2) % 2 ^ x)) * 2 + (me % 2 ^ c) for k, x, c in offsets]
    )

    def to_owners(columns):
        return lax.all_to_all(columns.T, "expert", split_axis=0, concat_axis=0, tiled=True)[sources]

    slots_here = to_owners(slots)
    select = {
        offset: (
            jnp.arange(capacity, dtype=jnp.int32)[:, None].astype(single_float)
            == slots_here[n][None, :]
        )
        for n, offset in enumerate(offsets)
    }
    cot_rows = gather_rows(cotangent, owners)
    full_in = whole_expert(expert_in[0])
    full_down = whole_expert(expert_down[0])
    resid_in = hidden.astype(single_float)
    inverse_one = lax.rsqrt(jnp.mean(resid_in * resid_in, axis=-1, keepdims=True) + norm_eps)
    normal_one = resid_in * inverse_one
    normed = (normal_one * gain_attn).astype(brain_float_half)
    query_pre = jnp.dot(normed, full_query, preferred_element_type=single_float)
    key_value_projected = jnp.dot(normed, full_keyval, preferred_element_type=single_float)
    cosine_lookup, sine_lookup = rotary_tables(sequence_length, HEAD_DIMENSION)
    query_rotated = apply_rotation(
        query_pre.reshape(sequence_length, QUERY_HEADS, HEAD_DIMENSION), cosine_lookup, sine_lookup
    ).astype(brain_float_half)
    key_rot = apply_rotation(
        key_value_projected[:, :key_columns].reshape(
            sequence_length, KEY_VALUE_HEADS, HEAD_DIMENSION
        ),
        cosine_lookup,
        sine_lookup,
    ).astype(brain_float_half)
    value_row_list = (
        key_value_projected[:, key_columns:]
        .reshape(sequence_length, KEY_VALUE_HEADS, HEAD_DIMENSION)
        .astype(brain_float_half)
    )
    block_length = min(512, sequence_length)
    block_total = sequence_length // block_length
    query_block_list = query_rotated.reshape(
        block_total, block_length, KEY_VALUE_HEADS, group_length, HEAD_DIMENSION
    )
    block_starts = jnp.arange(block_total, dtype=jnp.int32) * block_length

    def forward_block(pieces):
        query_block, block_start = pieces
        masked = masked_scores(query_block, key_rot, block_start, segments, scale)
        top_score = jnp.max(masked, axis=-1, keepdims=True)
        log_total = top_score + jnp.log(
            jnp.sum(jnp.exp(masked - top_score), axis=-1, keepdims=True)
        )
        prob_low = jnp.exp(masked - log_total).astype(brain_float_half)
        mixed = jnp.einsum(
            "kgqs,skd->qkgd", prob_low, value_row_list, preferred_element_type=single_float
        )
        return (mixed.astype(brain_float_half), log_total)

    attended_blocks, log_totals = lax.map(forward_block, (query_block_list, block_starts))
    attended = attended_blocks.reshape(sequence_length, QUERY_HEADS * HEAD_DIMENSION)
    first_sum = resid_in + jnp.dot(attended, full_out, preferred_element_type=single_float)
    inverse_two = lax.rsqrt(jnp.mean(first_sum * first_sum, axis=-1, keepdims=True) + norm_eps)
    normal_two = first_sum * inverse_two
    moe_in = (normal_two * gain_ffn).astype(brain_float_half)
    moe_rows = gather_rows(moe_in, owners)
    logits = jnp.dot(moe_in, full_router, preferred_element_type=single_float)
    gates = jax.nn.softmax(jnp.where(routed, logits, -jnp.inf), axis=-1)
    kept_gates = jnp.where(kept_mask, gates, 0.0)
    gates_here = to_owners(kept_gates)
    near_first = sorted(range(across), key=lambda k: min(k, across - k))
    split = max(1, across // 2)
    groups = [
        [(k, x, c) for k in part for x in range(2) for c in range(2)]
        for part in (near_first[:split], near_first[split:])
        if part
    ]
    out_parts, grad_parts, gate_parts = ({}, {}, {})
    in_part, down_part = (0.0, 0.0)
    for group in groups:
        pick = lambda rows: jnp.concatenate(
            [
                jnp.dot(
                    select[o].astype(brain_float_half), rows[o], preferred_element_type=single_float
                ).astype(brain_float_half)
                for o in group
            ],
            axis=0,
        )
        cot_here = pick(cot_rows)
        inputs_here = pick(moe_rows)
        slot_gate = jnp.concatenate(
            [
                jnp.sum(jnp.where(select[o], gates_here[offsets.index(o)][None, :], 0.0), axis=1)
                for o in group
            ]
        )[:, None]
        gate_up = jnp.dot(inputs_here, full_in, preferred_element_type=single_float)
        gate_part = gate_up[:, :FF]
        up_part = gate_up[:, FF:]
        sigmoid_g = jax.nn.sigmoid(gate_part)
        silu_g = gate_part * sigmoid_g
        expert_hidden = (silu_g * up_part).astype(brain_float_half)
        expert_out = jnp.einsum(
            "cf,df->cd", expert_hidden, full_down, preferred_element_type=single_float
        ).astype(brain_float_half)
        cot_single = cot_here.astype(single_float)
        slot_grad = jnp.sum(cot_single * expert_out.astype(single_float), axis=1)
        scaled_out = (expert_out.astype(single_float) * slot_gate).astype(brain_float_half)
        grad_rows = (cot_single * slot_gate).astype(brain_float_half)
        hidden_delta = jnp.dot(grad_rows, full_down, preferred_element_type=single_float)
        gate_delta = hidden_delta * up_part * sigmoid_g * (1.0 + gate_part * (1.0 - sigmoid_g))
        up_delta = hidden_delta * silu_g
        gate_up_grad = jnp.concatenate([gate_delta, up_delta], axis=-1).astype(brain_float_half)
        row_grads = jnp.einsum(
            "cf,df->cd", gate_up_grad, full_in, preferred_element_type=single_float
        ).astype(brain_float_half)
        down_part = down_part + jnp.einsum(
            "cd,cf->df", grad_rows, expert_hidden, preferred_element_type=single_float
        )
        in_part = in_part + jnp.einsum(
            "cd,cf->df", inputs_here, gate_up_grad, preferred_element_type=single_float
        )
        for n, o in enumerate(group):
            low = select[o].astype(brain_float_half)
            span = slice(n * capacity, (n + 1) * capacity)
            grad_parts[o] = jnp.einsum(
                "ct,cd->td", low, row_grads[span], preferred_element_type=single_float
            ).astype(brain_float_half)
            out_parts[o] = jnp.einsum(
                "ct,cd->td", low, scaled_out[span], preferred_element_type=single_float
            ).astype(brain_float_half)
            gate_parts[o] = jnp.sum(jnp.where(select[o], slot_grad[span][:, None], 0.0), axis=0)
    returned_gates = jnp.zeros((owners, sequence_length), single_float).at[sources].set(
        jnp.stack([gate_parts[o] for o in offsets]), unique_indices=True
    )
    gate_grad = lax.all_to_all(returned_gates, "expert", split_axis=0, concat_axis=0, tiled=True).T
    cot_value = cotangent.astype(single_float)
    select_grad = gates * (gate_grad - jnp.sum(gates * gate_grad, axis=-1, keepdims=True))
    logit_grad = select_grad.astype(brain_float_half)
    router_part = jnp.einsum("sd,se->ed", moe_in, logit_grad, preferred_element_type=single_float)
    moe_grad = jnp.einsum("se,de->sd", logit_grad, full_router, preferred_element_type=single_float)
    moe_grad = moe_grad + scatter_rows(grad_parts, owners)
    block_out = (first_sum + scatter_rows(out_parts, owners)).astype(brain_float_half)
    expert_in_share = fold_expert(in_part)[None]
    expert_down_share = fold_expert(down_part)[None]
    ffn_gain_part = jnp.sum(moe_grad * normal_two, axis=0)
    first_grad = cot_value + norm_backward(moe_grad, gain_ffn, normal_two, inverse_two)
    branch_grad = first_grad.astype(brain_float_half)
    out_part = jnp.einsum("sa,sd->ad", attended, branch_grad, preferred_element_type=single_float)
    attended_gradient = jnp.einsum(
        "sd,ad->sa", branch_grad, full_out, preferred_element_type=single_float
    ).astype(brain_float_half)
    gradient_blocks = attended_gradient.reshape(
        block_total, block_length, KEY_VALUE_HEADS, group_length, HEAD_DIMENSION
    )

    def backward_block(carry, pieces):
        key_acc, value_acc = carry
        query_block, grad_block, log_total, block_start = pieces
        masked = masked_scores(query_block, key_rot, block_start, segments, scale)
        probability = jnp.exp(masked - log_total)
        prob_low = probability.astype(brain_float_half)
        prob_grad = jnp.einsum(
            "qkgd,skd->kgqs", grad_block, value_row_list, preferred_element_type=single_float
        )
        row_dot = jnp.sum(probability * prob_grad, axis=-1, keepdims=True)
        score_grad = (probability * (prob_grad - row_dot)).astype(brain_float_half)
        query_delta = (
            jnp.einsum("kgqs,skd->qkgd", score_grad, key_rot, preferred_element_type=single_float)
            * scale
        )
        key_acc = (
            key_acc
            + jnp.einsum(
                "kgqs,qkgd->skd", score_grad, query_block, preferred_element_type=single_float
            )
            * scale
        )
        value_acc = value_acc + jnp.einsum(
            "kgqs,qkgd->skd", prob_low, grad_block, preferred_element_type=single_float
        )
        return ((key_acc, value_acc), query_delta)

    zeroed_rows = jnp.zeros((sequence_length, KEY_VALUE_HEADS, HEAD_DIMENSION), single_float)
    (key_delta, value_delta), query_deltas = lax.scan(
        backward_block,
        (zeroed_rows, zeroed_rows),
        (query_block_list, gradient_blocks, log_totals, block_starts),
    )
    query_grad_low = (
        unrotate(
            query_deltas.reshape(sequence_length, QUERY_HEADS, HEAD_DIMENSION),
            cosine_lookup,
            sine_lookup,
        )
        .astype(brain_float_half)
        .reshape(sequence_length, QUERY_HEADS * HEAD_DIMENSION)
    )
    key_grad_low = unrotate(key_delta, cosine_lookup, sine_lookup).reshape(
        sequence_length, key_columns
    )
    keyval_grad_low = jnp.concatenate(
        [key_grad_low, value_delta.reshape(sequence_length, key_columns)], axis=-1
    ).astype(brain_float_half)
    query_part = jnp.einsum(
        "sd,sa->da", normed, query_grad_low, preferred_element_type=single_float
    )
    keyval_part = jnp.einsum(
        "sd,sa->da", normed, keyval_grad_low, preferred_element_type=single_float
    )
    normed_grad = jnp.einsum(
        "sa,da->sd", query_grad_low, full_query, preferred_element_type=single_float
    )
    normed_grad = normed_grad + jnp.einsum(
        "sa,da->sd", keyval_grad_low, full_keyval, preferred_element_type=single_float
    )
    attn_gain_part = jnp.sum(normed_grad * normal_one, axis=0)
    hidden_grad = (
        first_grad + norm_backward(normed_grad, gain_attn, normal_one, inverse_one)
    ).astype(brain_float_half)
    side = lax.axis_index("dp")
    own = model_width // lax.axis_size("dp")
    early = lax.psum(
        jnp.concatenate([ffn_gain_part[None], router_part], axis=0), ("dp", "expert")
    )
    early = lax.dynamic_slice_in_dim(early, side * own, own, 1)
    late = lax.dynamic_slice_in_dim(lax.psum(attn_gain_part, ("dp", "expert")), side * own, own, 0)
    return (
        block_out,
        hidden_grad,
        late,
        fold_shared(query_part, owners),
        fold_shared(keyval_part, owners),
        fold_shared(out_part, owners),
        early[0],
        early[1:].T,
        expert_in_share,
        expert_down_share,
    )


def solution(mesh):
    placed = (
        P(("dp", "expert"), None),
        P(("dp", "expert")),
        P(("dp", "expert"), None),
        P(),
        P("dp"),
        P("dp", None),
        P("dp", None),
        P("dp", None),
        P("dp"),
        P("dp", None),
        P("expert", "dp", None),
        P("expert", "dp", None),
        P(("dp", "expert"), None),
    )
    return jax.shard_map(
        on_device,
        mesh=mesh,
        in_specs=placed,
        out_specs=(
            P(("dp", "expert"), None),
            P(("dp", "expert"), None),
            P("dp"),
            P("dp", None),
            P("dp", None),
            P("dp", None),
            P("dp"),
            P("dp", None),
            P("expert", "dp", None),
            P("expert", "dp", None),
        ),
        check_vma=False,
    )
```

```python
import jax
import jax.numpy as jnp
from jax import lax
from jax.sharding import PartitionSpec as P

QUERY_HEADS = 16
KEY_VALUE_HEADS = 8
HEAD_DIMENSION = 64
FF = 512
BLOCK_ROWS = 128
CB = 2


norm_eps = 1e-06
theta_base = 10000.0


def rotary_tables(sequence_length, head_dim):
    half_dim = head_dim // 2
    inverse = theta_base ** (-jnp.arange(half_dim, dtype=jnp.float32) * 2.0 / head_dim)
    angles = jnp.arange(sequence_length, dtype=jnp.float32)[:, None] * inverse[None, :]
    angles = jnp.concatenate([angles, angles], axis=-1)
    return (jnp.cos(angles), jnp.sin(angles))


def apply_rotation(value, cosine_lookup, sine_lookup):
    half_dim = value.shape[-1] // 2
    turned = jnp.concatenate([-value[..., half_dim:], value[..., :half_dim]], axis=-1)
    return value * cosine_lookup[:, None, :] + turned * sine_lookup[:, None, :]


def unrotate(grad_val, cosine_lookup, sine_lookup):
    half_dim = grad_val.shape[-1] // 2
    scaled = grad_val * sine_lookup[:, None, :]
    turned = jnp.concatenate([scaled[..., half_dim:], -scaled[..., :half_dim]], axis=-1)
    return grad_val * cosine_lookup[:, None, :] + turned


def masked_scores(query_block, key_rot, block_start, seg_ids, scale):
    span_len = query_block.shape[0]
    raw_scores = (
        jnp.einsum("qkgd,skd->kgqs", query_block, key_rot, preferred_element_type=jnp.float32)
        * scale
    )
    query_pos = block_start + jnp.arange(span_len, dtype=jnp.int32)
    key_pos = jnp.arange(key_rot.shape[0], dtype=jnp.int32)
    allowed = (query_pos[:, None] >= key_pos[None, :]) & (seg_ids[:, None] == seg_ids[None, :])
    return jnp.where(allowed[None, None], raw_scores, -1e30)


def norm_backward(grad_in, gain_vec, normalized, inverse_rms):
    scaled = grad_in * gain_vec
    return inverse_rms * (
        scaled - normalized * jnp.mean(scaled * normalized, axis=-1, keepdims=True)
    )


def at_offset(arr, owners, dz, dx, dc):
    pairs = []
    for i in range(owners):
        z, x, c = i // 4, (i // 2) % 2, i % 2
        source = (((z + dz) % (owners // 4)) * 2 + (x ^ dx)) * 2 + (c ^ dc)
        pairs.append((source, i))
    return lax.ppermute(arr, "expert", pairs)


def swap_dp(arr):
    return lax.ppermute(arr, "dp", [(0, 1), (1, 0)])


def piece(arr, index, size, axis=0):
    return lax.dynamic_slice_in_dim(arr, index * size, size, axis)


def in_order(first, mine, other, axis=0):
    return jnp.where(
        first, jnp.concatenate([mine, other], axis), jnp.concatenate([other, mine], axis)
    )


def add_low(left, right):
    return (left.astype(jnp.float32) + right.astype(jnp.float32)).astype(jnp.bfloat16)


def gather_rows(arr, owners):
    across = owners // 4
    got = {(0, 0, 0): arr}
    got[0, 1, 0] = at_offset(arr, owners, 0, 1, 0)
    order = sorted(range(1, across), key=lambda k: min(k, across - k))
    for k in order:
        got[k, 0, 0] = at_offset(arr, owners, k, 0, 0)
    for k in order:
        got[k, 1, 0] = at_offset(got[k, 0, 0], owners, 0, 1, 0)
    for k in [0] + order:
        for x in range(2):
            got[k, x, 1] = at_offset(got[k, x, 0], owners, 0, 0, 1)
    return got


def scatter_rows(parts, owners):
    across = owners // 4
    order = sorted(range(1, across), key=lambda k: min(k, across - k))
    total = None
    for k in order + [0]:
        far = add_low(parts[k, 1, 0], at_offset(parts[k, 1, 1], owners, 0, 0, 1))
        near = add_low(parts[k, 0, 0], at_offset(parts[k, 0, 1], owners, 0, 0, 1))
        row = add_low(near, at_offset(far, owners, 0, 1, 0))
        if k:
            row = at_offset(row, owners, across - k, 0, 0)
        row = row.astype(jnp.float32)
        total = row if total is None else total + row
    return total


def whole_rows(arr, owners):
    if lax.axis_size("dp") != 2:
        return lax.all_gather(arr, "dp", axis=0, tiled=True)
    core = lax.axis_index("expert") % 2
    got = swap_dp(piece(arr, core, arr.shape[0] // 2))
    other = in_order(core == 0, got, at_offset(got, owners, 0, 0, 1))
    return in_order(lax.axis_index("dp") == 0, arr, other)


def whole_expert(arr):
    if lax.axis_size("dp") != 2:
        return lax.all_gather(arr, "dp", axis=0, tiled=True)
    return in_order(lax.axis_index("dp") == 0, arr, swap_dp(arr))


def fold_expert(grad):
    if lax.axis_size("dp") != 2:
        return lax.psum_scatter(
            grad.astype(jnp.bfloat16), "dp", scatter_dimension=0, tiled=True
        ).astype(jnp.float32)
    side = lax.axis_index("dp")
    half = grad.shape[0] // 2
    sent = swap_dp(piece(grad, 1 - side, half).astype(jnp.bfloat16))
    return piece(grad, side, half) + sent.astype(jnp.float32)


def fold_shared(grad, owners):
    low = grad.astype(jnp.bfloat16)
    if lax.axis_size("dp") != 2:
        return lax.psum_scatter(
            lax.psum(low, "expert"), "dp", scatter_dimension=0, tiled=True
        ).astype(jnp.float32)
    me = lax.axis_index("expert")
    z, x, c = me // 4, (me // 2) % 2, me % 2
    side = lax.axis_index("dp")
    across = owners // 4
    wide = low.shape[1] // 2
    low = add_low(
        piece(low, c, wide, 1), at_offset(piece(low, 1 - c, wide, 1), owners, 0, 0, 1)
    )
    half = low.shape[0] // 2
    low = add_low(piece(low, side, half), swap_dp(piece(low, 1 - side, half)))
    quarter = half // 2
    low = add_low(piece(low, x, quarter), at_offset(piece(low, 1 - x, quarter), owners, 0, 1, 0))
    rows = quarter // across
    total = piece(low, z, rows).astype(jnp.float32)
    for k in range(1, across):
        sent = at_offset(piece(low, (z + across - k) % across, rows), owners, k, 0, 0)
        total = total + sent.astype(jnp.float32)
    low = total.astype(jnp.bfloat16)
    turned = [low] + [at_offset(low, owners, k, 0, 0) for k in range(1, across)]
    low = lax.dynamic_slice_in_dim(
        jnp.concatenate(turned + turned, 0), ((across - z) % across) * rows, quarter, 0
    )
    low = in_order(x == 0, low, at_offset(low, owners, 0, 1, 0))
    low = in_order(c == 0, low, at_offset(low, owners, 0, 0, 1), 1)
    return low.astype(jnp.float32)


def on_device(
    hidden,
    segments,
    routes,
    capacity_blocks,
    attn_gain,
    w_query,
    key_value_weight,
    w_out,
    ffn_gain,
    w_router,
    expert_in,
    expert_down,
    cotangent,
):
    sequence_length = hidden.shape[0]
    model_width = hidden.shape[1]
    expert_count = capacity_blocks.shape[0]
    owners = lax.axis_size("expert")
    across = owners // 4
    capacity = BLOCK_ROWS * CB
    group_length = QUERY_HEADS // KEY_VALUE_HEADS
    key_columns = KEY_VALUE_HEADS * HEAD_DIMENSION
    scale = HEAD_DIMENSION ** (-0.5)
    brain_float_half = jnp.bfloat16
    single_float = jnp.float32
    small = lax.all_gather(
        jnp.concatenate([attn_gain[None], ffn_gain[None], w_router.T], axis=0),
        "dp",
        axis=1,
        tiled=True,
    )
    gain_attn = small[0].astype(single_float)
    gain_ffn = small[1].astype(single_float)
    full_router = small[2:].T
    full_query = whole_rows(w_query, owners)
    full_keyval = whole_rows(key_value_weight, owners)
    full_out = whole_rows(w_out, owners)
    expert_ids = jnp.arange(expert_count, dtype=jnp.int32)
    routed = jnp.any(routes[:, :, None] == expert_ids[None, None, :], axis=1)
    earlier = (
        jnp.arange(sequence_length)[:, None] > jnp.arange(sequence_length)[None, :]
    ).astype(brain_float_half)
    ranks = jnp.dot(
        earlier, routed.astype(brain_float_half), preferred_element_type=single_float
    )
    kept_mask = routed & (ranks < (BLOCK_ROWS * capacity_blocks[None, :]).astype(single_float))
    slots = jnp.where(kept_mask, ranks, -1.0)
    me = lax.axis_index("expert")
    offsets = [(k, x, c) for k in range(across) for x in range(2) for c in range(2)]
    sources = jnp.stack(
        [(((me // 4 + k) % across) * 2 + ((me // 2) % 2 ^ x)) * 2 + (me % 2 ^ c) for k, x, c in offsets]
    )

    def to_owners(columns):
        return lax.all_to_all(columns.T, "expert", split_axis=0, concat_axis=0, tiled=True)[sources]

    slots_here = to_owners(slots)
    select = {
        offset: (
            jnp.arange(capacity, dtype=jnp.int32)[:, None].astype(single_float)
            == slots_here[n][None, :]
        )
        for n, offset in enumerate(offsets)
    }
    cot_all = lax.all_gather(cotangent, "expert", axis=0, tiled=True)
    cot_rows = {
        offset: piece(cot_all, sources[n], sequence_length) for n, offset in enumerate(offsets)
    }
    full_in = whole_expert(expert_in[0])
    full_down = whole_expert(expert_down[0])
    resid_in = hidden.astype(single_float)
    inverse_one = lax.rsqrt(jnp.mean(resid_in * resid_in, axis=-1, keepdims=True) + norm_eps)
    normal_one = resid_in * inverse_one
    normed = (normal_one * gain_attn).astype(brain_float_half)
    query_pre = jnp.dot(normed, full_query, preferred_element_type=single_float)
    key_value_projected = jnp.dot(normed, full_keyval, preferred_element_type=single_float)
    cosine_lookup, sine_lookup = rotary_tables(sequence_length, HEAD_DIMENSION)
    query_rotated = apply_rotation(
        query_pre.reshape(sequence_length, QUERY_HEADS, HEAD_DIMENSION), cosine_lookup, sine_lookup
    ).astype(brain_float_half)
    key_rot = apply_rotation(
        key_value_projected[:, :key_columns].reshape(
            sequence_length, KEY_VALUE_HEADS, HEAD_DIMENSION
        ),
        cosine_lookup,
        sine_lookup,
    ).astype(brain_float_half)
    value_row_list = (
        key_value_projected[:, key_columns:]
        .reshape(sequence_length, KEY_VALUE_HEADS, HEAD_DIMENSION)
        .astype(brain_float_half)
    )
    block_length = min(512, sequence_length)
    block_total = sequence_length // block_length
    query_block_list = query_rotated.reshape(
        block_total, block_length, KEY_VALUE_HEADS, group_length, HEAD_DIMENSION
    )
    block_starts = jnp.arange(block_total, dtype=jnp.int32) * block_length

    def forward_block(pieces):
        query_block, block_start = pieces
        masked = masked_scores(query_block, key_rot, block_start, segments, scale)
        top_score = jnp.max(masked, axis=-1, keepdims=True)
        log_total = top_score + jnp.log(
            jnp.sum(jnp.exp(masked - top_score), axis=-1, keepdims=True)
        )
        prob_low = jnp.exp(masked - log_total).astype(brain_float_half)
        mixed = jnp.einsum(
            "kgqs,skd->qkgd", prob_low, value_row_list, preferred_element_type=single_float
        )
        return (mixed.astype(brain_float_half), log_total)

    attended_blocks, log_totals = lax.map(forward_block, (query_block_list, block_starts))
    attended = attended_blocks.reshape(sequence_length, QUERY_HEADS * HEAD_DIMENSION)
    first_sum = resid_in + jnp.dot(attended, full_out, preferred_element_type=single_float)
    inverse_two = lax.rsqrt(jnp.mean(first_sum * first_sum, axis=-1, keepdims=True) + norm_eps)
    normal_two = first_sum * inverse_two
    moe_in = (normal_two * gain_ffn).astype(brain_float_half)
    moe_rows = gather_rows(moe_in, owners)
    logits = jnp.dot(moe_in, full_router, preferred_element_type=single_float)
    gates = jax.nn.softmax(jnp.where(routed, logits, -jnp.inf), axis=-1)
    kept_gates = jnp.where(kept_mask, gates, 0.0)
    gates_here = to_owners(kept_gates)
    near_first = sorted(range(across), key=lambda k: min(k, across - k))
    split = max(1, across // 2)
    groups = [
        [(k, x, c) for k in part for x in range(2) for c in range(2)]
        for part in (near_first[:split], near_first[split:])
        if part
    ]
    scaled_parts, grad_parts, gate_parts = ({}, {}, {})
    in_part, down_part = (0.0, 0.0)
    for group in groups:
        pick = lambda rows: jnp.concatenate(
            [
                jnp.dot(
                    select[o].astype(brain_float_half), rows[o], preferred_element_type=single_float
                ).astype(brain_float_half)
                for o in group
            ],
            axis=0,
        )
        cot_here = pick(cot_rows)
        inputs_here = pick(moe_rows)
        slot_gate = jnp.concatenate(
            [
                jnp.sum(jnp.where(select[o], gates_here[offsets.index(o)][None, :], 0.0), axis=1)
                for o in group
            ]
        )[:, None]
        gate_up = jnp.dot(inputs_here, full_in, preferred_element_type=single_float)
        gate_part = gate_up[:, :FF]
        up_part = gate_up[:, FF:]
        sigmoid_g = jax.nn.sigmoid(gate_part)
        silu_g = gate_part * sigmoid_g
        expert_hidden = (silu_g * up_part).astype(brain_float_half)
        expert_out = jnp.einsum(
            "cf,df->cd", expert_hidden, full_down, preferred_element_type=single_float
        ).astype(brain_float_half)
        cot_single = cot_here.astype(single_float)
        slot_grad = jnp.sum(cot_single * expert_out.astype(single_float), axis=1)
        scaled_out = (expert_out.astype(single_float) * slot_gate).astype(brain_float_half)
        grad_rows = (cot_single * slot_gate).astype(brain_float_half)
        hidden_delta = jnp.dot(grad_rows, full_down, preferred_element_type=single_float)
        gate_delta = hidden_delta * up_part * sigmoid_g * (1.0 + gate_part * (1.0 - sigmoid_g))
        up_delta = hidden_delta * silu_g
        gate_up_grad = jnp.concatenate([gate_delta, up_delta], axis=-1).astype(brain_float_half)
        row_grads = jnp.einsum(
            "cf,df->cd", gate_up_grad, full_in, preferred_element_type=single_float
        ).astype(brain_float_half)
        down_part = down_part + jnp.einsum(
            "cd,cf->df", grad_rows, expert_hidden, preferred_element_type=single_float
        )
        in_part = in_part + jnp.einsum(
            "cd,cf->df", inputs_here, gate_up_grad, preferred_element_type=single_float
        )
        for n, o in enumerate(group):
            low = select[o].astype(brain_float_half)
            span = slice(n * capacity, (n + 1) * capacity)
            grad_parts[o] = jnp.einsum(
                "ct,cd->td", low, row_grads[span], preferred_element_type=single_float
            ).astype(brain_float_half)
            scaled_parts[o] = scaled_out[span]
            gate_parts[o] = jnp.sum(jnp.where(select[o], slot_grad[span][:, None], 0.0), axis=0)
    returned_gates = jnp.zeros((owners, sequence_length), single_float).at[sources].set(
        jnp.stack([gate_parts[o] for o in offsets]), unique_indices=True
    )
    gate_grad = lax.all_to_all(returned_gates, "expert", split_axis=0, concat_axis=0, tiled=True).T
    cot_value = cotangent.astype(single_float)
    select_grad = gates * (gate_grad - jnp.sum(gates * gate_grad, axis=-1, keepdims=True))
    logit_grad = select_grad.astype(brain_float_half)
    router_part = jnp.einsum("sd,se->ed", moe_in, logit_grad, preferred_element_type=single_float)
    moe_grad = jnp.einsum("se,de->sd", logit_grad, full_router, preferred_element_type=single_float)
    moe_grad = moe_grad + scatter_rows(grad_parts, owners)
    places = jnp.zeros((owners,), jnp.int32).at[sources].set(
        jnp.arange(owners, dtype=jnp.int32), unique_indices=True
    )
    places, moe_grad = lax.optimization_barrier((places, moe_grad))
    scaled_all = jnp.stack([scaled_parts[o] for o in offsets])[places]
    select_all = (
        jnp.arange(capacity, dtype=jnp.int32)[None, :, None].astype(single_float)
        == slots_here[places][:, None, :]
    ).astype(brain_float_half)
    mixture = jnp.einsum(
        "nct,ncd->ntd", select_all, scaled_all, preferred_element_type=single_float
    ).astype(brain_float_half)
    mixture = lax.psum_scatter(mixture, "expert", scatter_dimension=0, tiled=True)[0]
    expert_in_share = fold_expert(in_part)[None]
    expert_down_share = fold_expert(down_part)[None]
    ffn_gain_part = jnp.sum(moe_grad * normal_two, axis=0)
    first_grad = cot_value + norm_backward(moe_grad, gain_ffn, normal_two, inverse_two)
    branch_grad = first_grad.astype(brain_float_half)
    out_part = jnp.einsum("sa,sd->ad", attended, branch_grad, preferred_element_type=single_float)
    attended_gradient = jnp.einsum(
        "sd,ad->sa", branch_grad, full_out, preferred_element_type=single_float
    ).astype(brain_float_half)
    gradient_blocks = attended_gradient.reshape(
        block_total, block_length, KEY_VALUE_HEADS, group_length, HEAD_DIMENSION
    )

    def backward_block(carry, pieces):
        key_acc, value_acc = carry
        query_block, grad_block, log_total, block_start = pieces
        masked = masked_scores(query_block, key_rot, block_start, segments, scale)
        probability = jnp.exp(masked - log_total)
        prob_low = probability.astype(brain_float_half)
        prob_grad = jnp.einsum(
            "qkgd,skd->kgqs", grad_block, value_row_list, preferred_element_type=single_float
        )
        row_dot = jnp.sum(probability * prob_grad, axis=-1, keepdims=True)
        score_grad = (probability * (prob_grad - row_dot)).astype(brain_float_half)
        query_delta = (
            jnp.einsum("kgqs,skd->qkgd", score_grad, key_rot, preferred_element_type=single_float)
            * scale
        )
        key_acc = (
            key_acc
            + jnp.einsum(
                "kgqs,qkgd->skd", score_grad, query_block, preferred_element_type=single_float
            )
            * scale
        )
        value_acc = value_acc + jnp.einsum(
            "kgqs,qkgd->skd", prob_low, grad_block, preferred_element_type=single_float
        )
        return ((key_acc, value_acc), query_delta)

    zeroed_rows = jnp.zeros((sequence_length, KEY_VALUE_HEADS, HEAD_DIMENSION), single_float)
    (key_delta, value_delta), query_deltas = lax.scan(
        backward_block,
        (zeroed_rows, zeroed_rows),
        (query_block_list, gradient_blocks, log_totals, block_starts),
    )
    query_grad_low = (
        unrotate(
            query_deltas.reshape(sequence_length, QUERY_HEADS, HEAD_DIMENSION),
            cosine_lookup,
            sine_lookup,
        )
        .astype(brain_float_half)
        .reshape(sequence_length, QUERY_HEADS * HEAD_DIMENSION)
    )
    key_grad_low = unrotate(key_delta, cosine_lookup, sine_lookup).reshape(
        sequence_length, key_columns
    )
    keyval_grad_low = jnp.concatenate(
        [key_grad_low, value_delta.reshape(sequence_length, key_columns)], axis=-1
    ).astype(brain_float_half)
    query_part = jnp.einsum(
        "sd,sa->da", normed, query_grad_low, preferred_element_type=single_float
    )
    keyval_part = jnp.einsum(
        "sd,sa->da", normed, keyval_grad_low, preferred_element_type=single_float
    )
    normed_grad = jnp.einsum(
        "sa,da->sd", query_grad_low, full_query, preferred_element_type=single_float
    )
    normed_grad = normed_grad + jnp.einsum(
        "sa,da->sd", keyval_grad_low, full_keyval, preferred_element_type=single_float
    )
    attn_gain_part = jnp.sum(normed_grad * normal_one, axis=0)
    hidden_grad = (
        first_grad + norm_backward(normed_grad, gain_attn, normal_one, inverse_one)
    ).astype(brain_float_half)
    mixture, hidden_grad = lax.optimization_barrier((mixture, hidden_grad))
    block_out = (first_sum + mixture.astype(single_float)).astype(brain_float_half)
    side = lax.axis_index("dp")
    own = model_width // lax.axis_size("dp")

    def total_small(rows):
        if lax.axis_size("dp") != 2:
            return lax.dynamic_slice_in_dim(lax.psum(rows, ("dp", "expert")), side * own, own, 1)
        rows = piece(rows, side, own, 1) + swap_dp(piece(rows, 1 - side, own, 1))
        copies = jnp.broadcast_to(rows[None], (owners,) + rows.shape)
        return jnp.sum(
            lax.all_to_all(copies, "expert", split_axis=0, concat_axis=0, tiled=True), axis=0
        )

    early = total_small(jnp.concatenate([ffn_gain_part[None], router_part], axis=0))
    late = total_small(attn_gain_part[None])[0]
    query_keyval = fold_shared(jnp.concatenate([query_part, keyval_part], axis=1), owners)
    query_share, keyval_share = (query_keyval[:, :model_width], query_keyval[:, model_width:])
    return (
        block_out,
        hidden_grad,
        late,
        query_share,
        keyval_share,
        fold_shared(out_part, owners),
        early[0],
        early[1:].T,
        expert_in_share,
        expert_down_share,
    )


def solution(mesh):
    placed = (
        P(("dp", "expert"), None),
        P(("dp", "expert")),
        P(("dp", "expert"), None),
        P(),
        P("dp"),
        P("dp", None),
        P("dp", None),
        P("dp", None),
        P("dp"),
        P("dp", None),
        P("expert", "dp", None),
        P("expert", "dp", None),
        P(("dp", "expert"), None),
    )
    return jax.shard_map(
        on_device,
        mesh=mesh,
        in_specs=placed,
        out_specs=(
            P(("dp", "expert"), None),
            P(("dp", "expert"), None),
            P("dp"),
            P("dp", None),
            P("dp", None),
            P("dp", None),
            P("dp"),
            P("dp", None),
            P("expert", "dp", None),
            P("expert", "dp", None),
        ),
        check_vma=False,
    )
```
